512 devices in a mesh: docs: 128 (over z_hi, y, x, core), proj: 4 (over z_lo).
Axes of the slice: x: 4, y: 4, z: 16 (z_hi: 4, z_lo: 4; z = z_hi * 4 + z_lo), core: 2. Of those that a mesh axis runs over, the one named last changes fastest.
Arguments:
- grads: bfloat16 [32768, 4096], P('docs', 'proj'), may hold values from -6 to 6
- precond: bfloat16 [4096, 4096], P('docs', 'proj'), may hold values from -3 to 3, as said below
- offsets: int32 [2], replicated, may hold values from 1 to 127
Outputs:
- influence: float32 [2, 32768, 256], P(None, 'docs')
The draws below stay inside these ranges and needn't reach their ends.
Inputs may be any that keep to these rules, and one draw needn't show every extreme that they name: `precond`: symmetric.
All inputs are finite; a program needn't handle non-finite values.
Results may differ from the reference program's by a relative error of at most 0.014.
Values may be sent and summed in bfloat16 or wider, within the bound.
No kernel may reach another device: no remote copies, remote signals or barrier semaphores. Data moves between devices by JAX's collectives and lax.ppermute only.
A program may use at most 64 MiB of HBM per device.

```python
import math
import jax
import jax.numpy as jnp
from jax import lax

K = 4096
DOC_DEV = 256
ROUNDS = 2
TOTAL = 32768
N_DOCS = 128


def draw_precond(key, part):
    key = jax.random.fold_in(key, 7)
    first, second = jax.random.split(key)
    base = jax.random.normal(first, (K, K), jnp.float32)
    diag_vals = jnp.exp(jax.random.uniform(second, (K,), jnp.float32, math.log(0.5), math.log(2.0)))
    sym = (base + base.T) * (0.5 / math.sqrt(2.0 * K))
    eye = jnp.eye(K, dtype=jnp.float32)
    return (sym + eye * diag_vals[:, None]).astype(jnp.bfloat16)


def levels(rng, extent, shards, low, high):
    def one(axis_at, parts):
        heights = jax.random.uniform(jax.random.fold_in(jax.random.fold_in(rng, 6), axis_at), (parts,), jnp.float32, low / len(shards), high / len(shards))
        return jnp.repeat(jnp.exp(heights), extent[axis_at] // parts).reshape((-1,) + (1,) * (len(extent) - axis_at - 1))

    factor_of = one(*shards[0])
    for cut in shards[1:]:
        factor_of = factor_of * one(*cut)
    return factor_of


def scatter_about(own_key, shape, width, reach, pieces=(), kind=jnp.bfloat16):
    entries = width * jax.random.normal(own_key, shape, jnp.float32)
    if pieces:
        entries = entries * levels(own_key, shape, pieces, -0.22, 0.18)
    return jnp.clip(entries, -reach, reach).astype(kind)


def setup_inputs(seed: int = 0) -> dict:
    key_list = jax.random.split(jax.random.key(seed), 4)
    grads = scatter_about(key_list[0], (TOTAL, K), 1.0, 6.0, ((0, 128), (1, 4)))
    precond = draw_precond(jax.random.fold_in(key_list[3], 71), 0)
    offsets = jax.random.randint(key_list[2], (ROUNDS,), 1, N_DOCS).astype(jnp.int32)
    return {"grads": grads, "precond": precond, "offsets": offsets}


def reference(grads, precond, offsets):
    blocks = grads.reshape(N_DOCS, DOC_DEV, K)

    def precondition(block):
        return jnp.dot(block, precond, preferred_element_type=jnp.float32).astype(jnp.bfloat16)
    pre = lax.map(precondition, blocks)
    factor = jnp.float32(1.0 / math.sqrt(K))
    results = []
    for step in range(ROUNDS):
        partner = jnp.roll(blocks, -offsets[step], axis=0)

        def block_gram(pair):
            return jnp.dot(pair[0], pair[1].T, preferred_element_type=jnp.float32) * factor
        grams = lax.map(block_gram, (pre, partner))
        results.append(grams.reshape(N_DOCS * DOC_DEV, DOC_DEV))
    return jnp.stack(results, axis=0)
```

```python
import math

import jax
import jax.numpy as jnp
from jax import lax
from jax.sharding import PartitionSpec as P

K = 4096
ROUNDS = 2
BOTH = ("docs", "proj")


def place(index):
    docs, p = divmod(index, 4)
    return docs >> 5, docs >> 3 & 3, docs >> 1 & 3, docs & 1, p


def number(zh, y, x, c, p):
    return ((zh % 4 * 4 + y % 4) * 4 + x % 4) * 8 + c % 2 * 4 + p % 4


def send(value, to):
    return lax.ppermute(value, BOTH, [(i, number(*to(*place(i)))) for i in range(512)])


def put(buffer, piece, at):
    return lax.dynamic_update_slice(
        buffer, piece[None], (at,) + (0,) * (buffer.ndim - 1)
    )


def gather4(value, mine, move):
    out = jnp.zeros((4,) + value.shape, value.dtype)
    out = put(out, value, mine)
    for t in (1, 2, 3):
        out = put(out, send(value, lambda *at: move(t, *at)), (mine - t) % 4)
    return out


def gather_precond(own):
    docs = lax.axis_index("docs")
    zh, y, x, c = docs >> 5, docs >> 3 & 3, docs >> 1 & 3, docs & 1
    held = gather4(own, zh, lambda t, zh, y, x, c, p: (zh + t, y, x, c, p))
    held = gather4(
        held,
        jnp.where(c == 0, y, x),
        lambda t, zh, y, x, c, p: (zh, y + t * (1 - c), x + t * c, c, p),
    )
    held = gather4(
        held,
        jnp.where(c == 0, x, y),
        lambda t, zh, y, x, c, p: (zh, y + t * c, x + t * (1 - c), c, p),
    )
    other = send(held, lambda zh, y, x, c, p: (zh, y, x, c ^ 1, p))
    first = jnp.where(c == 0, held, other).transpose(2, 1, 0, 3, 4)
    second = jnp.where(c == 0, other, held).transpose(2, 0, 1, 3, 4)
    return jnp.stack([first, second], axis=3).reshape(4096, own.shape[1])


def gather_grads(own):
    p = lax.axis_index("proj")
    parts = gather4(own, p, lambda t, zh, y, x, c, p: (zh, y, x, c, p + t))
    return [parts[i] for i in range(4)]


def sum_over_proj(part):
    p = lax.axis_index("proj")
    low = part.astype(jnp.bfloat16)

    def pick(array, at):
        return lax.dynamic_index_in_dim(array, at % 4, 0, keepdims=False)

    total = pick(part, p)
    for t in (1, 2, 3):
        got = send(pick(low, p + t), lambda zh, y, x, c, p: (zh, y, x, c, p + t))
        total = total + got.astype(jnp.float32)
    return gather4(
        total.astype(jnp.bfloat16), p, lambda t, zh, y, x, c, p: (zh, y, x, c, p + t)
    ).astype(jnp.float32)


def shifted(value, axis, by):
    size = lax.axis_size(axis)
    return lax.ppermute(value, axis, [(i, (i + by) % size) for i in range(size)])


def fetch_every(block, offset, bits_total):
    current = block
    for bit in range(bits_total):
        moved = shifted(current, "docs", -(1 << bit))
        current = jnp.where(offset >> bit & 1 == 1, moved, current)
    return current


def on_device(grads, precond, offsets):
    columns = gather_precond(precond)
    slabs = gather_grads(grads)
    pre = sum(
        jnp.dot(
            slabs[i],
            columns[i * 1024 : (i + 1) * 1024],
            preferred_element_type=jnp.float32,
        )
        for i in range(4)
    ).astype(jnp.bfloat16)
    factor = jnp.float32(1.0 / math.sqrt(K))
    bits_total = (lax.axis_size("docs") - 1).bit_length()
    grams = []
    for step in range(ROUNDS):
        partner = fetch_every(grads, offsets[step], bits_total)
        grams.append(
            lax.dot_general(
                pre, partner, (((1,), (1,)), ((), ())), preferred_element_type=jnp.float32
            )
        )
    whole = sum_over_proj(jnp.stack(grams).reshape(4, 128, 256))
    return whole.reshape(2, 256, 256) * factor


def solution(mesh):
    placed = (P("docs", "proj"), P("docs", "proj"), P())
    return jax.shard_map(
        on_device, mesh=mesh, in_specs=placed, out_specs=P(None, "docs", None), check_vma=False
    )
```

```python
import math

import jax
import jax.numpy as jnp
from jax import lax
from jax.sharding import PartitionSpec as P

K = 4096
ROUNDS = 2
BOTH = ("docs", "proj")
CHUNKS = 2


def place(index):
    docs, p = divmod(index, 4)
    return docs >> 5, docs >> 3 & 3, docs >> 1 & 3, docs & 1, p


def number(zh, y, x, c, p):
    return ((zh % 4 * 4 + y % 4) * 4 + x % 4) * 8 + c % 2 * 4 + p % 4


def send(value, to):
    return lax.ppermute(value, BOTH, [(i, number(*to(*place(i)))) for i in range(512)])


def put(buffer, piece, at):
    return lax.dynamic_update_slice(
        buffer, piece[None], (at,) + (0,) * (buffer.ndim - 1)
    )


def gather4(value, mine, move):
    out = jnp.zeros((4,) + value.shape, value.dtype)
    out = put(out, value, mine)
    for t in (1, 2, 3):
        out = put(out, send(value, lambda *at: move(t, *at)), (mine - t) % 4)
    return out


def gather_precond(own):
    docs = lax.axis_index("docs")
    zh, y, x, c = docs >> 5, docs >> 3 & 3, docs >> 1 & 3, docs & 1
    held = gather4(own, zh, lambda t, zh, y, x, c, p: (zh + t, y, x, c, p))
    held = gather4(
        held,
        jnp.where(c == 0, y, x),
        lambda t, zh, y, x, c, p: (zh, y + t * (1 - c), x + t * c, c, p),
    )
    held = gather4(
        held,
        jnp.where(c == 0, x, y),
        lambda t, zh, y, x, c, p: (zh, y + t * c, x + t * (1 - c), c, p),
    )
    other = send(held, lambda zh, y, x, c, p: (zh, y, x, c ^ 1, p))
    first = jnp.where(c == 0, held, other).transpose(2, 1, 0, 3, 4)
    second = jnp.where(c == 0, other, held).transpose(2, 0, 1, 3, 4)
    return jnp.stack([first, second], axis=3).reshape(4096, own.shape[1])


def sum_over_proj(part):
    p = lax.axis_index("proj")
    low = part.astype(jnp.bfloat16)

    def pick(array, at):
        return lax.dynamic_index_in_dim(array, at % 4, 0, keepdims=False)

    total = pick(part, p)
    for t in (1, 2, 3):
        got = send(pick(low, p + t), lambda zh, y, x, c, p: (zh, y, x, c, p + t))
        total = total + got.astype(jnp.float32)
    return gather4(
        total.astype(jnp.bfloat16), p, lambda t, zh, y, x, c, p: (zh, y, x, c, p + t)
    ).astype(jnp.float32)


def ring(value, by):
    def move(zh, y, x, c, p):
        z = 4 * zh + p + by
        return z // 4, y, x, c, z % 4

    out = []
    for _ in range(4):
        value = send(value, move)
        out.append(value)
    return out


def gather_grads(own):
    p = lax.axis_index("proj")
    rows = own.shape[0]
    step = rows // CHUNKS
    slabs, near = [], []
    for i in range(CHUNKS):
        chunk = own[i * step : (i + 1) * step]
        below = ring(chunk, 1)
        above = ring(chunk, -1)
        line = jnp.stack(below[2::-1] + [chunk] + above[:3])
        slabs.append(lax.dynamic_slice(line, (3 - p, 0, 0), (4,) + chunk.shape))
        near.append((above[3], below[3]))
    half = rows // 2
    up = jnp.concatenate([one[0] for one in near])
    down = jnp.concatenate([one[1] for one in near])
    far = jnp.concatenate(
        [
            send(up[:half], lambda zh, y, x, c, p: (zh - 1, y, x, c, p)),
            send(down[half:], lambda zh, y, x, c, p: (zh + 1, y, x, c, p)),
        ]
    )
    return jnp.concatenate(slabs, axis=1), jnp.stack([own, up, far, down])


def rotate(value, by):
    def branch(shift):
        def move(zh, y, x, c, p):
            m = (y * 8 + x * 2 + c - shift) % 32
            return zh, m >> 3, m >> 1 & 3, m & 1, p

        return lambda one: send(one, move) if shift else one

    return lax.switch(by, [branch(shift) for shift in range(32)], value)


def on_device(grads, precond, offsets):
    columns = gather_precond(precond)
    slabs, blocks = gather_grads(grads)
    pre = sum(
        jnp.dot(
            slabs[i],
            columns[i * 1024 : (i + 1) * 1024],
            preferred_element_type=jnp.float32,
        )
        for i in range(4)
    ).astype(jnp.bfloat16)
    factor = jnp.float32(1.0 / math.sqrt(K))
    m = lax.axis_index("docs") % 32
    grams = []
    for step in range(ROUNDS):
        low = offsets[step] % 32
        ahead = (offsets[step] // 32 + (m < low)) % 4
        partner = rotate(lax.dynamic_index_in_dim(blocks, ahead, 0, keepdims=False), low)
        grams.append(
            lax.dot_general(
                pre, partner, (((1,), (1,)), ((), ())), preferred_element_type=jnp.float32
            )
        )
    whole = sum_over_proj(jnp.stack(grams).reshape(4, 128, 256))
    return whole.reshape(2, 256, 256) * factor


def solution(mesh):
    placed = (P("docs", "proj"), P("docs", "proj"), P())
    return jax.shard_map(
        on_device, mesh=mesh, in_specs=placed, out_specs=P(None, "docs", None), check_vma=False
    )
```

```python
import math

import jax
import jax.numpy as jnp
from jax import lax
from jax.sharding import PartitionSpec as P

K = 4096
ROUNDS = 2
BOTH = ("docs", "proj")
CHUNKS = 2


def place(index):
    docs, p = divmod(index, 4)
    return docs >> 5, docs >> 3 & 3, docs >> 1 & 3, docs & 1, p


def number(zh, y, x, c, p):
    return ((zh % 4 * 4 + y % 4) * 4 + x % 4) * 8 + c % 2 * 4 + p % 4


def send(value, to):
    return lax.ppermute(value, BOTH, [(i, number(*to(*place(i)))) for i in range(512)])


def put(buffer, piece, at):
    return lax.dynamic_update_slice(
        buffer, piece[None], (at,) + (0,) * (buffer.ndim - 1)
    )


def gather4(value, mine, move):
    out = jnp.zeros((4,) + value.shape, value.dtype)
    out = put(out, value, mine)
    for t in (1, 2, 3):
        out = put(out, send(value, lambda *at: move(t, *at)), (mine - t) % 4)
    return out


def gather_precond(own):
    docs = lax.axis_index("docs")
    zh, y, x, c = docs >> 5, docs >> 3 & 3, docs >> 1 & 3, docs & 1
    held = gather4(own, zh, lambda t, zh, y, x, c, p: (zh + t, y, x, c, p))
    held = gather4(
        held,
        jnp.where(c == 0, y, x),
        lambda t, zh, y, x, c, p: (zh, y + t * (1 - c), x + t * c, c, p),
    )
    held = gather4(
        held,
        jnp.where(c == 0, x, y),
        lambda t, zh, y, x, c, p: (zh, y + t * c, x + t * (1 - c), c, p),
    )
    other = send(held, lambda zh, y, x, c, p: (zh, y, x, c ^ 1, p))
    first = jnp.where(c == 0, held, other).transpose(2, 1, 0, 3, 4)
    second = jnp.where(c == 0, other, held).transpose(2, 0, 1, 3, 4)
    return jnp.stack([first, second], axis=3).reshape(4096, own.shape[1])


def sum_over_proj(part):
    p = lax.axis_index("proj")
    low = part.astype(jnp.bfloat16)

    def pick(array, at):
        return lax.dynamic_index_in_dim(array, at % 4, 0, keepdims=False)

    total = pick(part, p)
    for t in (1, 2, 3):
        got = send(pick(low, p + t), lambda zh, y, x, c, p: (zh, y, x, c, p + t))
        total = total + got.astype(jnp.float32)
    return gather4(
        total.astype(jnp.bfloat16), p, lambda t, zh, y, x, c, p: (zh, y, x, c, p + t)
    ).astype(jnp.float32)


def ring(value, by):
    def move(zh, y, x, c, p):
        z = 4 * zh + p + by
        return z // 4, y, x, c, z % 4

    out = []
    for _ in range(4):
        value = send(value, move)
        out.append(value)
    return out


def gather_grads(own):
    p = lax.axis_index("proj")
    rows = own.shape[0]
    step = rows // CHUNKS
    slabs, near = [], []
    for i in range(CHUNKS):
        chunk = own[i * step : (i + 1) * step]
        below = ring(chunk, 1)
        above = ring(chunk, -1)
        line = jnp.stack(below[2::-1] + [chunk] + above[:3])
        slabs.append(lax.dynamic_slice(line, (3 - p, 0, 0), (4,) + chunk.shape))
        near.append((above[3], below[3]))
    half = rows // 2
    up = jnp.concatenate([one[0] for one in near])
    down = jnp.concatenate([one[1] for one in near])
    far = jnp.concatenate(
        [
            send(up[:half], lambda zh, y, x, c, p: (zh - 1, y, x, c, p)),
            send(down[half:], lambda zh, y, x, c, p: (zh + 1, y, x, c, p)),
        ]
    )
    return jnp.concatenate(slabs, axis=1), jnp.stack([own, up, far, down])


def rotate(value, by):
    def turn(one, shift):
        def move(zh, y, x, c, p):
            m = (y * 8 + x * 2 + c - shift) % 32
            return zh, m >> 3, m >> 1 & 3, m & 1, p

        return send(one, move) if shift else one

    def branch(shift):
        return lambda one: turn(turn(one, shift % 2), shift - shift % 2)

    return lax.switch(by, [branch(shift) for shift in range(32)], value)


def on_device(grads, precond, offsets):
    columns = gather_precond(precond)
    slabs, blocks = gather_grads(grads)
    pre = sum(
        jnp.dot(
            slabs[i],
            columns[i * 1024 : (i + 1) * 1024],
            preferred_element_type=jnp.float32,
        )
        for i in range(4)
    ).astype(jnp.bfloat16)
    factor = jnp.float32(1.0 / math.sqrt(K))
    m = lax.axis_index("docs") % 32
    grams = []
    for step in range(ROUNDS):
        low = offsets[step] % 32
        ahead = (offsets[step] // 32 + (m < low)) % 4
        partner = rotate(lax.dynamic_index_in_dim(blocks, ahead, 0, keepdims=False), low)
        grams.append(
            lax.dot_general(
                pre, partner, (((1,), (1,)), ((), ())), preferred_element_type=jnp.float32
            )
        )
    whole = sum_over_proj(jnp.stack(grams).reshape(4, 128, 256))
    return whole.reshape(2, 256, 256) * factor


def solution(mesh):
    placed = (P("docs", "proj"), P("docs", "proj"), P())
    return jax.shard_map(
        on_device, mesh=mesh, in_specs=placed, out_specs=P(None, "docs", None), check_vma=False
    )
```

```python
import math

import jax
import jax.numpy as jnp
from jax import lax
from jax.sharding import PartitionSpec as P

K = 4096
BOTH = ("docs", "proj")


def place(index):
    docs, p = divmod(index, 4)
    return docs >> 5, docs >> 3 & 3, docs >> 1 & 3, docs & 1, p


def number(zh, y, x, c, p):
    return ((zh % 4 * 4 + y % 4) * 4 + x % 4) * 8 + c % 2 * 4 + p % 4


def send(value, to):
    return lax.ppermute(value, BOTH, [(i, number(*to(*place(i)))) for i in range(512)])


def tied(first, second):
    return lax.optimization_barrier((first, second))


def put(buffer, piece, at):
    return lax.dynamic_update_slice(
        buffer, piece[None], (at,) + (0,) * (buffer.ndim - 1)
    )


def gather4(value, mine, move):
    out = jnp.zeros((4,) + value.shape, value.dtype)
    out = put(out, value, mine)
    for t in (1, 2, 3):
        out = put(out, send(value, lambda *at: move(t, *at)), (mine - t) % 4)
    return out


def along_zh(t, zh, y, x, c, p):
    return zh + t, y, x, c, p


def along_first(t, zh, y, x, c, p):
    return zh, y + t * (1 - c), x + t * c, c, p


def along_second(t, zh, y, x, c, p):
    return zh, y + t * c, x + t * (1 - c), c, p


def up_z(zh, y, x, c, p):
    z = 4 * zh + p + 1
    return z // 4, y, x, c, z % 4


def down_z(zh, y, x, c, p):
    z = 4 * zh + p - 1
    return z // 4, y, x, c, z % 4


def rotate(value, by, extra):
    def turn(one, shift):
        def move(zh, y, x, c, p):
            m = (y * 8 + x * 2 + c - shift) % 32
            return zh, m >> 3, m >> 1 & 3, m & 1, p

        return send(one, move) if shift else one

    def branch(shift):
        def run(one, more):
            return turn(turn(one, shift % 2), shift - shift % 2), exchange(more)

        return run

    return lax.switch(by, [branch(shift) for shift in range(32)], value, extra)


def exchange(part):
    if part is None:
        return None
    return [
        send(part, lambda zh, y, x, c, p: (zh, y, x, c, p + t)) for t in (1, 2, 3)
    ]


def total(part, others):
    for other in others:
        part = part + other.astype(jnp.float32)
    return part * jnp.float32(1.0 / math.sqrt(K))


def on_device(grads, precond, offsets):
    docs, p = lax.axis_index("docs"), lax.axis_index("proj")
    zh, y, x, c = docs >> 5, docs >> 3 & 3, docs >> 1 & 3, docs & 1
    m = docs % 32

    below, above = [send(grads, up_z)], [send(grads, down_z)]
    held = gather4(precond, (zh - p) % 4, along_zh)
    held, step = tied(held, (below[0], above[0]))
    below.append(send(step[0], up_z))
    above.append(send(step[1], down_z))
    held = gather4(held, jnp.where(c == 0, y, x), along_first)
    held, step = tied(held, (below[1], above[1]))
    below.append(send(step[0], up_z))
    above.append(send(step[1], down_z))
    held = gather4(held, jnp.where(c == 0, x, y), along_second)
    below.append(send(below[2], up_z))
    above.append(send(above[2], down_z))
    held, step = tied(held, (below[3], above[3]))
    below[3], above[3] = step
    other = send(held, lambda zh, y, x, c, p: (zh, y, x, c ^ 1, p))

    half = grads.shape[0] // 2
    far = jnp.concatenate(
        [
            send(above[3][:half], lambda *at: along_zh(-1, *at)),
            send(below[3][half:], lambda *at: along_zh(1, *at)),
        ]
    )

    first = jnp.where(c == 0, held, other).transpose(2, 1, 0, 3, 4)
    second = jnp.where(c == 0, other, held).transpose(2, 0, 1, 3, 4)
    rows = jnp.stack([first, second], axis=3).reshape(4, 1024, precond.shape[1])
    slabs = [grads] + [
        jnp.where(p + i < 4, above[i - 1], below[3 - i]) for i in (1, 2, 3)
    ]
    pre = sum(
        jnp.dot(slabs[i], rows[i], preferred_element_type=jnp.float32) for i in range(4)
    ).astype(jnp.bfloat16)
    far, pre = tied(far, pre)

    blocks = [grads, above[3], far, below[3]]

    def partner(round_, extra):
        low = offsets[round_] % 32
        ahead = (offsets[round_] // 32 + (m < low)) % 4
        value = blocks[0]
        for i in (1, 2, 3):
            value = jnp.where(ahead == i, blocks[i], value)
        return rotate(value, low, extra)

    def gram(other):
        return lax.dot_general(
            pre, other, (((1,), (1,)), ((), ())), preferred_element_type=jnp.float32
        )

    one = gram(partner(0, None)[0])
    moved, ones = partner(1, one.astype(jnp.bfloat16))
    two = gram(moved)
    twos = exchange(two.astype(jnp.bfloat16))
    return jnp.stack([total(one, ones), total(two, twos)])


def solution(mesh):
    placed = (P("docs", "proj"), P("docs", "proj"), P())
    return jax.shard_map(
        on_device, mesh=mesh, in_specs=placed, out_specs=P(None, "docs", None), check_vma=False
    )
```

```python
import math

import jax
import jax.numpy as jnp
from jax import lax
from jax.sharding import PartitionSpec as P

K = 4096
BOTH = ("docs", "proj")


def place(index):
    docs, p = divmod(index, 4)
    return docs >> 5, docs >> 3 & 3, docs >> 1 & 3, docs & 1, p


def number(zh, y, x, c, p):
    return ((zh % 4 * 4 + y % 4) * 4 + x % 4) * 8 + c % 2 * 4 + p % 4


def send(value, to):
    return lax.ppermute(value, BOTH, [(i, number(*to(*place(i)))) for i in range(512)])


def after(value, *others):
    return lax.optimization_barrier((value,) + others)[0]


def put(buffer, piece, at):
    return lax.dynamic_update_slice(
        buffer, piece[None], (at,) + (0,) * (buffer.ndim - 1)
    )


def gather4(value, mine, move):
    out = jnp.zeros((4,) + value.shape, value.dtype)
    out = put(out, value, mine)
    for t in (1, 2, 3):
        out = put(out, send(value, lambda *at: move(t, *at)), (mine - t) % 4)
    return out


def along_zh(t, zh, y, x, c, p):
    return zh + t, y, x, c, p


def groups(key):
    found = {}
    for docs in range(128):
        found.setdefault(key(*place(4 * docs)[:4]), []).append(docs)
    return list(found.values())


FIRST = groups(lambda zh, y, x, c: (zh, c, y if c else x))
SECOND = groups(lambda zh, y, x, c: (zh, c, x if c else y))
CORES = groups(lambda zh, y, x, c: (zh, y, x))


def gather(value, which):
    return lax.all_gather(value, "docs", axis_index_groups=which)


def up_z(zh, y, x, c, p):
    z = 4 * zh + p + 1
    return z // 4, y, x, c, z % 4


def down_z(zh, y, x, c, p):
    z = 4 * zh + p - 1
    return z // 4, y, x, c, z % 4


def rotate(value, by):
    def branch(shift):
        def move(zh, y, x, c, p):
            m = (y * 8 + x * 2 + c - shift) % 32
            return zh, m >> 3, m >> 1 & 3, m & 1, p

        return lambda one: send(one, move) if shift else one

    return lax.switch(by, [branch(shift) for shift in range(32)], value)


def on_device(grads, precond, offsets):
    docs, p = lax.axis_index("docs"), lax.axis_index("proj")
    zh, m = docs // 32, docs % 32

    below, above = [grads], [grads]
    for _ in range(4):
        below.append(send(below[-1], up_z))
        above.append(send(above[-1], down_z))
    held = gather4(precond, (zh - p) % 4, along_zh)
    for step, which in ((1, FIRST), (2, SECOND), (4, CORES)):
        held = gather(after(held, below[step], above[step]), which)

    half = grads.shape[0] // 2
    far = jnp.concatenate(
        [
            send(above[4][:half], lambda *at: along_zh(-1, *at)),
            send(below[4][half:], lambda *at: along_zh(1, *at)),
        ]
    )
    blocks = [grads, above[4], far, below[4]]

    def partner(round_):
        low = offsets[round_] % 32
        ahead = (offsets[round_] // 32 + (m < low)) % 4
        value = blocks[0]
        for i in (1, 2, 3):
            value = jnp.where(ahead == i, blocks[i], value)
        return rotate(value, low)

    partners = [partner(0), partner(1)]

    rows = jnp.stack(
        [held[0].transpose(2, 1, 0, 3, 4), held[1].transpose(2, 0, 1, 3, 4)], axis=3
    ).reshape(4, 1024, precond.shape[1])
    slabs = [grads] + [
        jnp.where(p + i < 4, above[i], below[4 - i]) for i in (1, 2, 3)
    ]
    pre = sum(
        jnp.dot(slabs[i], rows[i], preferred_element_type=jnp.float32) for i in range(4)
    ).astype(jnp.bfloat16)
    grams = jnp.stack(
        [
            lax.dot_general(
                pre, other, (((1,), (1,)), ((), ())), preferred_element_type=jnp.float32
            )
            for other in partners
        ]
    )
    parts = lax.all_gather(grams.astype(jnp.bfloat16), "proj").astype(jnp.float32)
    return jnp.sum(parts, axis=0) * jnp.float32(1.0 / math.sqrt(K))


def solution(mesh):
    placed = (P("docs", "proj"), P("docs", "proj"), P())
    return jax.shard_map(
        on_device, mesh=mesh, in_specs=placed, out_specs=P(None, "docs", None), check_vma=False
    )
```

```python
import math

import jax
import jax.numpy as jnp
from jax import lax
from jax.sharding import PartitionSpec as P

K = 4096
BOTH = ("docs", "proj")
SPLIT = (17, 19, 21, 23, 25, 27, 29, 31)


def place(index):
    docs, p = divmod(index, 4)
    return docs >> 5, docs >> 3 & 3, docs >> 1 & 3, docs & 1, p


def number(zh, y, x, c, p):
    return ((zh % 4 * 4 + y % 4) * 4 + x % 4) * 8 + c % 2 * 4 + p % 4


def send(value, to):
    return lax.ppermute(value, BOTH, [(i, number(*to(*place(i)))) for i in range(512)])


def after(value, *others):
    return lax.optimization_barrier((value,) + others)[0]


def put(buffer, piece, at):
    return lax.dynamic_update_slice(
        buffer, piece[None], (at,) + (0,) * (buffer.ndim - 1)
    )


def gather4(value, mine, move, *others):
    out = jnp.zeros((4,) + value.shape, value.dtype)
    out = put(out, value, mine)
    for t in (1, 3, 2):
        if t == 2 and others:
            value = after(value, *others)
        out = put(out, send(value, lambda *at: move(t, *at)), (mine - t) % 4)
    return out


def along_zh(t, zh, y, x, c, p):
    return zh + t, y, x, c, p


def along_first(t, zh, y, x, c, p):
    return zh, y + t * (1 - c), x + t * c, c, p


def along_second(t, zh, y, x, c, p):
    return zh, y + t * c, x + t * (1 - c), c, p


def up_z(zh, y, x, c, p):
    z = 4 * zh + p + 1
    return z // 4, y, x, c, z % 4


def down_z(zh, y, x, c, p):
    z = 4 * zh + p - 1
    return z // 4, y, x, c, z % 4


def rotate(value, by, work=None, *operands):
    def turn(one, shift):
        def move(zh, y, x, c, p):
            m = (y * 8 + x * 2 + c - shift) % 32
            return zh, m >> 3, m >> 1 & 3, m & 1, p

        return send(one, move) if shift else one

    def branch(shift):
        parts = (1, shift - 1) if shift in SPLIT else (shift,)

        def run(one, *more):
            for part in parts:
                one = turn(one, part)
            return (one, work(*more)) if work else one

        return run

    return lax.switch(by, [branch(shift) for shift in range(32)], value, *operands)


def sum_over_proj(part):
    pieces = part.astype(jnp.bfloat16).reshape((4, -1) + part.shape[-1:])
    mine = jnp.sum(
        lax.all_to_all(pieces, "proj", 0, 0).astype(jnp.float32), axis=0
    ).astype(jnp.bfloat16)
    every = lax.all_to_all(jnp.broadcast_to(mine, (4,) + mine.shape), "proj", 0, 0)
    return every.astype(jnp.float32).reshape(part.shape)


def on_device(grads, precond, offsets):
    docs, p = lax.axis_index("docs"), lax.axis_index("proj")
    zh, y, x, c = docs >> 5, docs >> 3 & 3, docs >> 1 & 3, docs & 1
    m = docs % 32

    below, above = [grads], [grads]
    for _ in range(4):
        below.append(send(below[-1], up_z))
        above.append(send(above[-1], down_z))
    slabs = [grads] + [
        jnp.where(p + i < 4, above[i], below[4 - i]) for i in (1, 2, 3)
    ]
    held = gather4(precond, (zh - p) % 4, along_zh, below[1], above[1])
    held = after(held, slabs[2])
    held = gather4(held, jnp.where(c == 0, y, x), along_first)
    held = after(held, slabs[1], slabs[3])
    held = gather4(held, jnp.where(c == 0, x, y), along_second)
    held = after(held, below[4], above[4])
    other = send(held, lambda zh, y, x, c, p: (zh, y, x, c ^ 1, p))

    half = grads.shape[0] // 2
    far = jnp.concatenate(
        [
            send(above[4][:half], lambda *at: along_zh(-1, *at)),
            send(below[4][half:], lambda *at: along_zh(1, *at)),
        ]
    )
    blocks = [grads, above[4], far, below[4]]

    def partner(round_, *work):
        low = offsets[round_] % 32
        ahead = (offsets[round_] // 32 + (m < low)) % 4
        value = blocks[0]
        for i in (1, 2, 3):
            value = jnp.where(ahead == i, blocks[i], value)
        return rotate(value, low, *work)

    def precondition(slabs, held, other):
        first = jnp.where(c == 0, held, other).transpose(2, 1, 0, 3, 4)
        second = jnp.where(c == 0, other, held).transpose(2, 0, 1, 3, 4)
        rows = jnp.stack([first, second], axis=3).reshape(4, 1024, precond.shape[1])
        return sum(
            jnp.dot(slab, part, preferred_element_type=jnp.float32)
            for slab, part in zip(slabs, rows)
        ).astype(jnp.bfloat16)

    one = partner(0)
    two, pre = partner(1, precondition, slabs, held, other)
    grams = jnp.stack(
        [
            lax.dot_general(
                pre, moved, (((1,), (1,)), ((), ())), preferred_element_type=jnp.float32
            )
            for moved in (one, two)
        ]
    )
    return sum_over_proj(grams) * jnp.float32(1.0 / math.sqrt(K))


def solution(mesh):
    placed = (P("docs", "proj"), P("docs", "proj"), P())
    return jax.shard_map(
        on_device, mesh=mesh, in_specs=placed, out_specs=P(None, "docs", None), check_vma=False
    )
```

```python
import math

import jax
import jax.numpy as jnp
from jax import lax
from jax.sharding import PartitionSpec as P

K = 4096
BOTH = ("docs", "proj")
SPLIT = (17, 19, 21, 23, 25, 27, 29, 31)


def place(index):
    docs, p = divmod(index, 4)
    return docs >> 5, docs >> 3 & 3, docs >> 1 & 3, docs & 1, p


def number(zh, y, x, c, p):
    return ((zh % 4 * 4 + y % 4) * 4 + x % 4) * 8 + c % 2 * 4 + p % 4


def send(value, to):
    return lax.ppermute(value, BOTH, [(i, number(*to(*place(i)))) for i in range(512)])


def put(buffer, piece, at):
    return lax.dynamic_update_slice(
        buffer, piece[None], (at,) + (0,) * (buffer.ndim - 1)
    )


def gather4(value, mine, move):
    out = jnp.zeros((4,) + value.shape, value.dtype)
    out = put(out, value, mine)
    for t in (1, 3, 2):
        out = put(out, send(value, lambda *at: move(t, *at)), (mine - t) % 4)
    return out


def along_zh(t, zh, y, x, c, p):
    return zh + t, y, x, c, p


def along_first(t, zh, y, x, c, p):
    return zh, y + t * (1 - c), x + t * c, c, p


def along_second(t, zh, y, x, c, p):
    return zh, y + t * c, x + t * (1 - c), c, p


def up_z(zh, y, x, c, p):
    z = 4 * zh + p + 1
    return z // 4, y, x, c, z % 4


def down_z(zh, y, x, c, p):
    z = 4 * zh + p - 1
    return z // 4, y, x, c, z % 4


def rotate(value, by):
    def turn(one, shift):
        def move(zh, y, x, c, p):
            m = (y * 8 + x * 2 + c - shift) % 32
            return zh, m >> 3, m >> 1 & 3, m & 1, p

        return send(one, move) if shift else one

    def branch(shift):
        if shift in SPLIT:
            return lambda one: turn(turn(one, 1), shift - 1)
        return lambda one: turn(one, shift)

    return lax.switch(by, [branch(shift) for shift in range(32)], value)


def sum_over_proj(part):
    pieces = part.astype(jnp.bfloat16).reshape((4, -1) + part.shape[-1:])
    mine = jnp.sum(
        lax.all_to_all(pieces, "proj", 0, 0).astype(jnp.float32), axis=0
    ).astype(jnp.bfloat16)
    every = lax.all_to_all(jnp.broadcast_to(mine, (4,) + mine.shape), "proj", 0, 0)
    return every.astype(jnp.float32).reshape(part.shape)


def on_device(grads, precond, offsets):
    docs, p = lax.axis_index("docs"), lax.axis_index("proj")
    zh, y, x, c = docs >> 5, docs >> 3 & 3, docs >> 1 & 3, docs & 1
    m = docs % 32

    below, above = [grads], [grads]

    def step():
        below.append(send(below[-1], up_z))
        above.append(send(above[-1], down_z))

    def meet(rows):
        rows, below[-1], above[-1] = lax.optimization_barrier(
            (rows, below[-1], above[-1])
        )
        return rows

    step()
    held = meet(gather4(precond, (zh - p) % 4, along_zh))
    step()
    held = meet(gather4(held, jnp.where(c == 0, y, x), along_first))
    step()
    held = gather4(held, jnp.where(c == 0, x, y), along_second)
    step()
    held = meet(held)
    other = send(held, lambda zh, y, x, c, p: (zh, y, x, c ^ 1, p))

    half = grads.shape[0] // 2
    far = jnp.concatenate(
        [
            send(above[4][:half], lambda *at: along_zh(-1, *at)),
            send(below[4][half:], lambda *at: along_zh(1, *at)),
        ]
    )
    first = jnp.where(c == 0, held, other).transpose(2, 1, 0, 3, 4)
    second = jnp.where(c == 0, other, held).transpose(2, 0, 1, 3, 4)
    rows = jnp.stack([first, second], axis=3).reshape(4, 1024, precond.shape[1])
    slabs = [grads] + [
        jnp.where(p + i < 4, above[i], below[4 - i]) for i in (1, 2, 3)
    ]
    pre = sum(
        jnp.dot(slab, part, preferred_element_type=jnp.float32)
        for slab, part in zip(slabs, rows)
    ).astype(jnp.bfloat16)
    far, pre = lax.optimization_barrier((far, pre))
    blocks = [grads, above[4], far, below[4]]

    grams = []
    for offset in (offsets[0], offsets[1]):
        low = offset % 32
        ahead = (offset // 32 + (m < low)) % 4
        value = blocks[0]
        for i in (1, 2, 3):
            value = jnp.where(ahead == i, blocks[i], value)
        grams.append(
            lax.dot_general(
                pre,
                rotate(value, low),
                (((1,), (1,)), ((), ())),
                preferred_element_type=jnp.float32,
            )
        )
    return sum_over_proj(jnp.stack(grams)) * jnp.float32(1.0 / math.sqrt(K))


def solution(mesh):
    placed = (P("docs", "proj"), P("docs", "proj"), P())
    return jax.shard_map(
        on_device, mesh=mesh, in_specs=placed, out_specs=P(None, "docs", None), check_vma=False
    )
```

```python
import math

import jax
import jax.numpy as jnp
from jax import lax
from jax.sharding import PartitionSpec as P

K = 4096
BOTH = ("docs", "proj")
SPLIT = (17, 19, 21, 23, 25, 27, 29, 31)


def place(index):
    docs, p = divmod(index, 4)
    return docs >> 5, docs >> 3 & 3, docs >> 1 & 3, docs & 1, p


def number(zh, y, x, c, p):
    return ((zh % 4 * 4 + y % 4) * 4 + x % 4) * 8 + c % 2 * 4 + p % 4


def send(value, to):
    return lax.ppermute(value, BOTH, [(i, number(*to(*place(i)))) for i in range(512)])


def put(buffer, piece, at):
    return lax.dynamic_update_slice(
        buffer, piece[None], (at,) + (0,) * (buffer.ndim - 1)
    )


def gather4(value, mine, move):
    out = jnp.zeros((4,) + value.shape, value.dtype)
    out = put(out, value, mine)
    for t in (1, 3, 2):
        out = put(out, send(value, lambda *at: move(t, *at)), (mine - t) % 4)
    return out


def gather_zh(value, mine):
    out = jnp.zeros((4,) + value.shape, value.dtype)
    out = put(out, value, mine)
    for t in (3, 1, 1):
        got = send(value, lambda *at: along_zh(t, *at))
        if t == 1:
            value, mine = got, mine - 1
            out = put(out, got, mine % 4)
        else:
            out = put(out, got, (mine - t) % 4)
    return out


def along_zh(t, zh, y, x, c, p):
    return zh + t, y, x, c, p


def along_first(t, zh, y, x, c, p):
    return zh, y + t * (1 - c), x + t * c, c, p


def along_second(t, zh, y, x, c, p):
    return zh, y + t * c, x + t * (1 - c), c, p


def up_z(zh, y, x, c, p):
    z = 4 * zh + p + 1
    return z // 4, y, x, c, z % 4


def down_z(zh, y, x, c, p):
    z = 4 * zh + p - 1
    return z // 4, y, x, c, z % 4


def rotate(value, by, *more):
    def turn(one, shift):
        def move(zh, y, x, c, p):
            m = (y * 8 + x * 2 + c - shift) % 32
            return zh, m >> 3, m >> 1 & 3, m & 1, p

        return send(one, move) if shift else one

    def branch(shift):
        def run(one, *more):
            if shift in SPLIT:
                one = turn(turn(one, 1), shift - 1)
            else:
                one = turn(one, shift)
            return one, [spread(other) for other in more]

        return run

    return lax.switch(by, [branch(shift) for shift in range(32)], value, *more)


def spread(part):
    return lax.all_to_all(jnp.broadcast_to(part, (4,) + part.shape), "proj", 0, 0)


def total(parts):
    return jnp.sum(parts.astype(jnp.float32), axis=0) * jnp.float32(1.0 / math.sqrt(K))


def on_device(grads, precond, offsets):
    docs, p = lax.axis_index("docs"), lax.axis_index("proj")
    zh, y, x, c = docs >> 5, docs >> 3 & 3, docs >> 1 & 3, docs & 1
    m = docs % 32

    below, above = [grads], [grads]

    def step():
        below.append(send(below[-1], up_z))
        above.append(send(above[-1], down_z))

    def meet(rows):
        rows, below[-1], above[-1] = lax.optimization_barrier(
            (rows, below[-1], above[-1])
        )
        return rows

    step()
    held = meet(gather_zh(precond, (zh - p) % 4))
    step()
    held = meet(gather4(held, jnp.where(c == 0, y, x), along_first))
    step()
    held = gather4(held, jnp.where(c == 0, x, y), along_second)
    step()
    held = meet(held)
    other = send(held, lambda zh, y, x, c, p: (zh, y, x, c ^ 1, p))

    half = grads.shape[0] // 2
    low_half = send(above[4][:half], lambda *at: along_zh(-1, *at))
    high_half = send(below[4][half:], lambda *at: along_zh(1, *at))

    first = jnp.where(c == 0, held, other).transpose(2, 1, 0, 3, 4)
    second = jnp.where(c == 0, other, held).transpose(2, 0, 1, 3, 4)
    rows = jnp.stack([first, second], axis=3).reshape(4, 1024, precond.shape[1])
    slabs = [grads] + [
        jnp.where(p + i < 4, above[i], below[4 - i]) for i in (1, 2, 3)
    ]
    pre = sum(
        jnp.dot(slab, part, preferred_element_type=jnp.float32)
        for slab, part in zip(slabs, rows)
    ).astype(jnp.bfloat16)
    low_half, high_half, pre = lax.optimization_barrier((low_half, high_half, pre))
    blocks = [grads, above[4], jnp.concatenate([low_half, high_half]), below[4]]

    def chosen(offset):
        low = offset % 32
        ahead = (offset // 32 + (m < low)) % 4
        value = blocks[0]
        for i in (1, 2, 3):
            value = jnp.where(ahead == i, blocks[i], value)
        return value, low

    def gram(other):
        return lax.dot_general(
            pre, other, (((1,), (1,)), ((), ())), preferred_element_type=jnp.float32
        ).astype(jnp.bfloat16)

    moved, _ = rotate(*chosen(offsets[0]))
    moved, (ones,) = rotate(*chosen(offsets[1]), gram(moved))
    twos = spread(gram(moved))
    return jnp.stack([total(ones), total(twos)])


def solution(mesh):
    placed = (P("docs", "proj"), P("docs", "proj"), P())
    return jax.shard_map(
        on_device, mesh=mesh, in_specs=placed, out_specs=P(None, "docs", None), check_vma=False
    )
```

```python
import math

import jax
import jax.numpy as jnp
from jax import lax
from jax.sharding import PartitionSpec as P

K = 4096
BOTH = ("docs", "proj")


def place(index):
    docs, p = divmod(index, 4)
    return docs >> 5, docs >> 3 & 3, docs >> 1 & 3, docs & 1, p


def number(zh, y, x, c, p):
    return ((zh % 4 * 4 + y % 4) * 4 + x % 4) * 8 + c % 2 * 4 + p % 4


def send(value, to):
    return lax.ppermute(value, BOTH, [(i, number(*to(*place(i)))) for i in range(512)])


def put(buffer, piece, at):
    return lax.dynamic_update_slice(
        buffer, piece[None], (at,) + (0,) * (buffer.ndim - 1)
    )


def groups(key):
    found = {}
    for docs in range(128):
        found.setdefault(key(*place(4 * docs)[:4]), []).append(docs)
    return list(found.values())


FIRST = groups(lambda zh, y, x, c: (zh, c, y if c else x))
SECOND = groups(lambda zh, y, x, c: (zh, c, x if c else y))


def spread(part, axis="proj", which=None):
    parts = jnp.broadcast_to(part, (4,) + part.shape)
    return lax.all_to_all(parts, axis, 0, 0, axis_index_groups=which)


def gather_zh(value, mine):
    out = jnp.zeros((4,) + value.shape, value.dtype)
    out = put(out, value, mine)
    for t in (3, 1, 1):
        got = send(value, lambda *at: along_zh(t, *at))
        if t == 1:
            value, mine = got, mine - 1
            out = put(out, got, mine % 4)
        else:
            out = put(out, got, (mine - t) % 4)
    return out


def along_zh(t, zh, y, x, c, p):
    return zh + t, y, x, c, p


def up_z(zh, y, x, c, p):
    z = 4 * zh + p + 1
    return z // 4, y, x, c, z % 4


def down_z(zh, y, x, c, p):
    z = 4 * zh + p - 1
    return z // 4, y, x, c, z % 4


def rotate(value, by):
    def turn(one, shift):
        def move(zh, y, x, c, p):
            m = (y * 8 + x * 2 + c - shift) % 32
            return zh, m >> 3, m >> 1 & 3, m & 1, p

        return send(one, move) if shift else one

    def branch(shift):
        if shift == 31:
            return lambda one: turn(turn(one, 1), 30)
        return lambda one: turn(one, shift)

    return lax.switch(by, [branch(shift) for shift in range(32)], value)


def sum_over_proj(part):
    pieces = part.astype(jnp.bfloat16).reshape((4, -1) + part.shape[-1:])
    mine = jnp.sum(
        lax.all_to_all(pieces, "proj", 0, 0).astype(jnp.float32), axis=0
    ).astype(jnp.bfloat16)
    return spread(mine).astype(jnp.float32).reshape(part.shape)


def on_device(grads, precond, offsets):
    docs, p = lax.axis_index("docs"), lax.axis_index("proj")
    zh, c, m = docs // 32, docs % 2, docs % 32
    picks = [
        (offset % 32, (offset // 32 + (m < offset % 32)) % 4)
        for offset in (offsets[0], offsets[1])
    ]

    below, above = [grads], [grads]

    def step():
        below.append(send(below[-1], up_z))
        above.append(send(above[-1], down_z))

    def meet(rows):
        rows, below[-1], above[-1] = lax.optimization_barrier(
            (rows, below[-1], above[-1])
        )
        return rows

    step()
    picks, below[1] = lax.optimization_barrier((picks, below[1]))
    held = meet(gather_zh(precond, (zh - p) % 4))
    step()
    held = meet(spread(held, "docs", FIRST))
    step()
    held = spread(held, "docs", SECOND)
    step()
    held = meet(held)
    other = send(held, lambda zh, y, x, c, p: (zh, y, x, c ^ 1, p))

    half = grads.shape[0] // 2
    low_half = send(above[4][:half], lambda *at: along_zh(-1, *at))
    high_half = send(below[4][half:], lambda *at: along_zh(1, *at))

    first = jnp.where(c == 0, held, other).transpose(2, 1, 0, 3, 4)
    second = jnp.where(c == 0, other, held).transpose(2, 0, 1, 3, 4)
    rows = jnp.stack([first, second], axis=3).reshape(4, 1024, precond.shape[1])
    slabs = [grads] + [
        jnp.where(p + i < 4, above[i], below[4 - i]) for i in (1, 2, 3)
    ]
    pre = sum(
        jnp.dot(slab, part, preferred_element_type=jnp.float32)
        for slab, part in zip(slabs, rows)
    ).astype(jnp.bfloat16)
    low_half, high_half, pre = lax.optimization_barrier((low_half, high_half, pre))
    blocks = [grads, above[4], jnp.concatenate([low_half, high_half]), below[4]]

    def chosen(low, ahead):
        value = blocks[0]
        for i in (1, 2, 3):
            value = jnp.where(ahead == i, blocks[i], value)
        return value, low

    grams = [
        lax.dot_general(
            pre,
            rotate(*chosen(*where)),
            (((1,), (1,)), ((), ())),
            preferred_element_type=jnp.float32,
        )
        for where in picks
    ]
    return sum_over_proj(jnp.stack(grams)) * jnp.float32(1.0 / math.sqrt(K))


def solution(mesh):
    placed = (P("docs", "proj"), P("docs", "proj"), P())
    return jax.shard_map(
        on_device, mesh=mesh, in_specs=placed, out_specs=P(None, "docs", None), check_vma=False
    )
```

```python
import math

import jax
import jax.numpy as jnp
from jax import lax
from jax.sharding import PartitionSpec as P

K = 4096
BOTH = ("docs", "proj")
SPLIT = (19, 21, 23, 25, 27, 29, 31)


def place(index):
    docs, p = divmod(index, 4)
    return docs >> 5, docs >> 3 & 3, docs >> 1 & 3, docs & 1, p


def number(zh, y, x, c, p):
    return ((zh % 4 * 4 + y % 4) * 4 + x % 4) * 8 + c % 2 * 4 + p % 4


def send(value, to):
    return lax.ppermute(value, BOTH, [(i, number(*to(*place(i)))) for i in range(512)])


def put(buffer, piece, at):
    return lax.dynamic_update_slice(
        buffer, piece[None], (at,) + (0,) * (buffer.ndim - 1)
    )


def gather4(value, mine, move):
    out = jnp.zeros((4,) + value.shape, value.dtype)
    out = put(out, value, mine)
    for t in (1, 3, 2):
        out = put(out, send(value, lambda *at: move(t, *at)), (mine - t) % 4)
    return out


def gather_zh(value, mine):
    out = jnp.zeros((4,) + value.shape, value.dtype)
    out = put(out, value, mine)
    for t in (3, 1, 1):
        got = send(value, lambda *at: along_zh(t, *at))
        if t == 1:
            value, mine = got, mine - 1
            out = put(out, got, mine % 4)
        else:
            out = put(out, got, (mine - t) % 4)
    return out


def along_zh(t, zh, y, x, c, p):
    return zh + t, y, x, c, p


def along_first(t, zh, y, x, c, p):
    return zh, y + t * (1 - c), x + t * c, c, p


def along_second(t, zh, y, x, c, p):
    return zh, y + t * c, x + t * (1 - c), c, p


def up_z(zh, y, x, c, p):
    z = 4 * zh + p + 1
    return z // 4, y, x, c, z % 4


def down_z(zh, y, x, c, p):
    z = 4 * zh + p - 1
    return z // 4, y, x, c, z % 4


def rotate(value, by):
    def turn(one, shift):
        def move(zh, y, x, c, p):
            m = (y * 8 + x * 2 + c - shift) % 32
            return zh, m >> 3, m >> 1 & 3, m & 1, p

        return send(one, move) if shift else one

    def branch(shift):
        if shift in SPLIT:
            return lambda one: turn(turn(one, 1), shift - 1)
        return lambda one: turn(one, shift % 32)

    return lax.switch(by, [branch(shift) for shift in range(33)], value)


def sum_over_proj(part):
    pieces = part.astype(jnp.bfloat16).reshape((4, -1) + part.shape[-1:])
    mine = jnp.sum(
        lax.all_to_all(pieces, "proj", 0, 0).astype(jnp.float32), axis=0
    ).astype(jnp.bfloat16)
    every = lax.all_to_all(jnp.broadcast_to(mine, (4,) + mine.shape), "proj", 0, 0)
    return every.astype(jnp.float32).reshape(part.shape)


def on_device(grads, precond, offsets):
    docs, p = lax.axis_index("docs"), lax.axis_index("proj")
    zh, y, x, c = docs >> 5, docs >> 3 & 3, docs >> 1 & 3, docs & 1
    m = docs % 32
    lows = [offsets[0] % 32, offsets[1] % 32]
    turns = [offsets[0] // 32, offsets[1] // 32]
    needs = [(turn == 2) | ((turn == 1) & (low > 0)) for low, turn in zip(lows, turns)]
    both, swap = needs[0] & needs[1], needs[0] & ~needs[1]
    low = [jnp.where(swap, lows[1], lows[0]), jnp.where(swap, lows[0], lows[1])]
    turn = [jnp.where(swap, turns[1], turns[0]), jnp.where(swap, turns[0], turns[1])]
    ahead = [(turn[i] + (m < low[i])) % 4 for i in (0, 1)]
    ways = [jnp.where(both, 32, low[0]), jnp.where(both, low[0], 32), low[1]]

    below, above = [grads], [grads]

    def step():
        below.append(send(below[-1], up_z))
        above.append(send(above[-1], down_z))

    def meet(rows):
        rows, below[-1], above[-1] = lax.optimization_barrier(
            (rows, below[-1], above[-1])
        )
        return rows

    step()
    ahead, ways, swap, both, below[1] = lax.optimization_barrier(
        (ahead, ways, swap, both, below[1])
    )
    held = meet(gather_zh(precond, (zh - p) % 4))
    step()
    held = meet(gather4(held, jnp.where(c == 0, y, x), along_first))
    step()
    held = gather4(held, jnp.where(c == 0, x, y), along_second)
    step()
    held = meet(held)
    other = send(held, lambda zh, y, x, c, p: (zh, y, x, c ^ 1, p))

    half = grads.shape[0] // 2
    low_half = send(above[4][:half], lambda *at: along_zh(-1, *at))
    high_half = send(below[4][half:], lambda *at: along_zh(1, *at))

    first = jnp.where(c == 0, held, other).transpose(2, 1, 0, 3, 4)
    second = jnp.where(c == 0, other, held).transpose(2, 0, 1, 3, 4)
    rows = jnp.stack([first, second], axis=3).reshape(4, 1024, precond.shape[1])
    slabs = [grads] + [
        jnp.where(p + i < 4, above[i], below[4 - i]) for i in (1, 2, 3)
    ]
    pre = sum(
        jnp.dot(slab, part, preferred_element_type=jnp.float32)
        for slab, part in zip(slabs, rows)
    ).astype(jnp.bfloat16)

    def chosen(which, far):
        value = grads
        for i, block in ((1, above[4]), (2, far), (3, below[4])):
            if block is not None:
                value = jnp.where(ahead[which] == i, block, value)
        return value

    one = rotate(chosen(0, None), ways[0])
    low_half, high_half, pre, one = lax.optimization_barrier(
        (low_half, high_half, pre, one)
    )
    far = jnp.concatenate([low_half, high_half])
    one = rotate(jnp.where(both, chosen(0, far), one), ways[1])
    two = rotate(chosen(1, far), ways[2])
    grams = [
        lax.dot_general(
            pre, partner, (((1,), (1,)), ((), ())), preferred_element_type=jnp.float32
        )
        for partner in (one, two)
    ]
    parts = [jnp.where(swap, grams[1], grams[0]), jnp.where(swap, grams[0], grams[1])]
    return sum_over_proj(jnp.stack(parts)) * jnp.float32(1.0 / math.sqrt(K))


def solution(mesh):
    placed = (P("docs", "proj"), P("docs", "proj"), P())
    return jax.shard_map(
        on_device, mesh=mesh, in_specs=placed, out_specs=P(None, "docs", None), check_vma=False
    )
```

```python
import math

import jax
import jax.numpy as jnp
from jax import lax
from jax.sharding import PartitionSpec as P

K = 4096
BOTH = ("docs", "proj")
SPLIT = (19, 21, 23, 25, 27, 29, 31)


def place(index):
    docs, p = divmod(index, 4)
    return docs >> 5, docs >> 3 & 3, docs >> 1 & 3, docs & 1, p


def number(zh, y, x, c, p):
    return ((zh % 4 * 4 + y % 4) * 4 + x % 4) * 8 + c % 2 * 4 + p % 4


def send(value, to):
    return lax.ppermute(value, BOTH, [(i, number(*to(*place(i)))) for i in range(512)])


def put(buffer, piece, at):
    return lax.dynamic_update_slice(
        buffer, piece[None], (at,) + (0,) * (buffer.ndim - 1)
    )


def gather4(value, mine, move):
    out = jnp.zeros((4,) + value.shape, value.dtype)
    out = put(out, value, mine)
    for t in (1, 3, 2):
        out = put(out, send(value, lambda *at: move(t, *at)), (mine - t) % 4)
    return out


def gather_zh(value, mine):
    out = jnp.zeros((4,) + value.shape, value.dtype)
    out = put(out, value, mine)
    for t in (3, 1, 1):
        got = send(value, lambda *at: along_zh(t, *at))
        if t == 1:
            value, mine = got, mine - 1
            out = put(out, got, mine % 4)
        else:
            out = put(out, got, (mine - t) % 4)
    return out


def along_zh(t, zh, y, x, c, p):
    return zh + t, y, x, c, p


def along_first(t, zh, y, x, c, p):
    return zh, y + t * (1 - c), x + t * c, c, p


def along_second(t, zh, y, x, c, p):
    return zh, y + t * c, x + t * (1 - c), c, p


def up_z(zh, y, x, c, p):
    z = 4 * zh + p + 1
    return z // 4, y, x, c, z % 4


def down_z(zh, y, x, c, p):
    z = 4 * zh + p - 1
    return z // 4, y, x, c, z % 4


def rotate(value, by):
    def turn(one, shift):
        def move(zh, y, x, c, p):
            m = (y * 8 + x * 2 + c - shift) % 32
            return zh, m >> 3, m >> 1 & 3, m & 1, p

        return send(one, move) if shift else one

    def branch(shift):
        if shift in SPLIT:
            return lambda one: turn(turn(one, 1), shift - 1)
        return lambda one: turn(one, shift % 32)

    return lax.switch(by, [branch(shift) for shift in range(33)], value)


def sum_over_proj(part):
    pieces = part.astype(jnp.bfloat16).reshape((4, -1) + part.shape[-1:])
    mine = jnp.sum(
        lax.all_to_all(pieces, "proj", 0, 0).astype(jnp.float32), axis=0
    ).astype(jnp.bfloat16)
    every = lax.all_to_all(jnp.broadcast_to(mine, (4,) + mine.shape), "proj", 0, 0)
    return every.astype(jnp.float32).reshape(part.shape)


def on_device(grads, precond, offsets):
    docs, p = lax.axis_index("docs"), lax.axis_index("proj")
    zh, y, x, c = docs >> 5, docs >> 3 & 3, docs >> 1 & 3, docs & 1
    m = docs % 32
    lows = [offsets[0] % 32, offsets[1] % 32]
    turns = [offsets[0] // 32, offsets[1] // 32]
    needs = [(turn == 2) | ((turn == 1) & (low > 0)) for low, turn in zip(lows, turns)]
    both, swap = needs[0] & needs[1], needs[0] & ~needs[1]
    low = [jnp.where(swap, lows[1], lows[0]), jnp.where(swap, lows[0], lows[1])]
    turn = [jnp.where(swap, turns[1], turns[0]), jnp.where(swap, turns[0], turns[1])]
    ahead = [(turn[i] + (m < low[i])) % 4 for i in (0, 1)]
    ways = [jnp.where(both, 32, low[0]), jnp.where(both, low[0], 32), low[1]]

    below, above = [grads], [grads]

    def step():
        below.append(send(below[-1], up_z))
        above.append(send(above[-1], down_z))

    def meet(rows):
        rows, below[-1], above[-1] = lax.optimization_barrier(
            (rows, below[-1], above[-1])
        )
        return rows

    step()
    ahead, ways, swap, both, below[1] = lax.optimization_barrier(
        (ahead, ways, swap, both, below[1])
    )
    step()
    held = meet(gather_zh(precond, (zh - p) % 4))
    step()
    held = meet(gather4(held, jnp.where(c == 0, y, x), along_first))
    step()
    held = meet(gather4(held, jnp.where(c == 0, x, y), along_second))
    other = send(held, lambda zh, y, x, c, p: (zh, y, x, c ^ 1, p))

    half = grads.shape[0] // 2
    low_half = send(above[4][:half], lambda *at: along_zh(-1, *at))
    high_half = send(below[4][half:], lambda *at: along_zh(1, *at))

    first = jnp.where(c == 0, held, other).transpose(2, 1, 0, 3, 4)
    second = jnp.where(c == 0, other, held).transpose(2, 0, 1, 3, 4)
    rows = jnp.stack([first, second], axis=3).reshape(4, 1024, precond.shape[1])
    slabs = [grads] + [
        jnp.where(p + i < 4, above[i], below[4 - i]) for i in (1, 2, 3)
    ]
    pre = sum(
        jnp.dot(slab, part, preferred_element_type=jnp.float32)
        for slab, part in zip(slabs, rows)
    ).astype(jnp.bfloat16)

    def chosen(which, far):
        value = grads
        for i, block in ((1, above[4]), (2, far), (3, below[4])):
            if block is not None:
                value = jnp.where(ahead[which] == i, block, value)
        return value

    one = rotate(chosen(0, None), ways[0])
    low_half, high_half, pre, one = lax.optimization_barrier(
        (low_half, high_half, pre, one)
    )
    far = jnp.concatenate([low_half, high_half])
    one = rotate(jnp.where(both, chosen(0, far), one), ways[1])
    two = rotate(chosen(1, far), ways[2])
    grams = [
        lax.dot_general(
            pre, partner, (((1,), (1,)), ((), ())), preferred_element_type=jnp.float32
        )
        for partner in (one, two)
    ]
    parts = [jnp.where(swap, grams[1], grams[0]), jnp.where(swap, grams[0], grams[1])]
    return sum_over_proj(jnp.stack(parts)) * jnp.float32(1.0 / math.sqrt(K))


def solution(mesh):
    placed = (P("docs", "proj"), P("docs", "proj"), P())
    return jax.shard_map(
        on_device, mesh=mesh, in_specs=placed, out_specs=P(None, "docs", None), check_vma=False
    )
```
